256 devices in a mesh: grp: 8 (over x_hi, y), sp: 32 (over x_lo, z, core).
Axes of the slice: x: 4 (x_hi: 2, x_lo: 2; x = x_hi * 2 + x_lo), y: 4, z: 8, core: 2. Of those that a mesh axis runs over, the one named last changes fastest.
Arguments:
- queries: bfloat16 [32768, 8192], P(('grp', 'sp')), may hold values from -160 to 160
- keys: bfloat16 [32768, 1024], P(('grp', 'sp')), may hold values from -6 to 6
- values: bfloat16 [32768, 1024], P(('grp', 'sp')), may hold values from -6 to 6
Outputs:
- attended: bfloat16 [32768, 8192], P(('grp', 'sp'))
The draws below stay inside these ranges and needn't reach their ends.
All inputs are finite; a program needn't handle non-finite values.
Results may differ from the reference program's by a relative error of at most 0.008.
Values may be sent and summed in bfloat16 or wider, within the bound.
A program may use at most 64 MiB of HBM per device.

```python
import jax
import jax.numpy as jnp
from jax import lax

QUERY_HEADS = 64
KEY_VALUE_HEADS = 8
HEAD_SIZE = 128
BLOCK_TOKENS = 1024
CONTEXT_TOKENS = 32768


def common_keys(key):
    unrotated_keys = jax.random.normal(jax.random.fold_in(key, 11), (CONTEXT_TOKENS, KEY_VALUE_HEADS, HEAD_SIZE), jnp.float32)
    return jnp.clip(unrotated_keys, -6.0, 6.0)


def draw_keys(key, part):
    anchor_shared_prefix = common_keys(key)
    return anchor_shared_prefix.reshape(CONTEXT_TOKENS, KEY_VALUE_HEADS * HEAD_SIZE).astype(jnp.bfloat16)


def draw_queries(key, part):
    key = jax.random.fold_in(key, 5)
    drawn = jnp.clip(jax.random.normal(key, (CONTEXT_TOKENS, QUERY_HEADS, HEAD_SIZE), jnp.float32), -6.0, 6.0)
    return drawn.reshape(CONTEXT_TOKENS, QUERY_HEADS * HEAD_SIZE).astype(jnp.bfloat16)


def block_levels(rng, shape, split, least, top_value):
    gain = 1.0
    for dim, blocks in split:
        heights = jax.random.uniform(jax.random.fold_in(jax.random.fold_in(rng, 6), dim), (blocks,), jnp.float32, least / len(split), top_value / len(split))
        gain = gain * jnp.repeat(jnp.exp(heights), shape[dim] // blocks).reshape((-1,) + (1,) * (len(shape) - 1 - dim))
    return gain


def bell_draw(rng, extent, width, most, cuts=(), held_as=jnp.bfloat16):
    gain = block_levels(rng, extent, cuts, -0.22, 0.18) if cuts else 1.0
    result = jax.random.normal(rng, extent, jnp.float32) * width * gain
    return jnp.minimum(jnp.maximum(result, -most), most).astype(held_as)


def setup_inputs(seed: int = 0) -> dict:
    seeds = jax.random.split(jax.random.key(seed), 4)
    queries = draw_queries(jax.random.fold_in(seeds[3], 71), 0)
    keys = draw_keys(jax.random.fold_in(seeds[3], 71), 0)
    values = bell_draw(seeds[2], (CONTEXT_TOKENS, KEY_VALUE_HEADS * HEAD_SIZE), 1.0, 6.0, ((0, 256),))
    return {"queries": queries, "keys": keys, "values": values}


def reference(queries, keys, values):
    grouped_query_rows = QUERY_HEADS // KEY_VALUE_HEADS
    context_block_count = CONTEXT_TOKENS // BLOCK_TOKENS
    score_scale = HEAD_SIZE ** -0.5
    blockwise_queries = queries.reshape(context_block_count, BLOCK_TOKENS, KEY_VALUE_HEADS, grouped_query_rows, HEAD_SIZE)
    blockwise_keys = keys.reshape(context_block_count, BLOCK_TOKENS, KEY_VALUE_HEADS, HEAD_SIZE)
    blockwise_values = values.reshape(context_block_count, BLOCK_TOKENS, KEY_VALUE_HEADS, HEAD_SIZE)
    anchor_k = blockwise_keys[0].astype(jnp.float32)
    anchor_v = blockwise_values[0].astype(jnp.float32)
    rows = jnp.arange(BLOCK_TOKENS)
    causal = rows[:, None] >= rows[None, :]

    def attend_block(items):
        query_block, key_block, value_block, block_index = items
        query_wide = query_block.astype(jnp.float32)
        local_scores = jnp.einsum("qhgd,khd->hgqk", query_wide, key_block.astype(jnp.float32)) * score_scale
        local_scores = jnp.where(causal, local_scores, -1e30)
        anchor_scores = jnp.einsum("qhgd,khd->hgqk", query_wide, anchor_k) * score_scale
        anchor_scores = jnp.where(block_index > 0, anchor_scores, -1e30)
        top_score = jnp.maximum(jnp.max(local_scores, axis=-1), jnp.max(anchor_scores, axis=-1))
        local_weights = jnp.exp(local_scores - top_score[..., None])
        anchor_weights = jnp.exp(anchor_scores - top_score[..., None])
        total = jnp.sum(local_weights, axis=-1) + jnp.sum(anchor_weights, axis=-1)
        local_rounded = lax.optimization_barrier(local_weights.astype(jnp.bfloat16))
        anchor_rounded = lax.optimization_barrier(anchor_weights.astype(jnp.bfloat16))
        summed = jnp.einsum("hgqk,khd->qhgd", local_rounded.astype(jnp.float32), value_block.astype(jnp.float32))
        summed = summed + jnp.einsum("hgqk,khd->qhgd", anchor_rounded.astype(jnp.float32), anchor_v)
        return (summed / jnp.transpose(total, (2, 0, 1))[..., None]).astype(jnp.bfloat16)

    outputs = lax.map(attend_block, (blockwise_queries, blockwise_keys, blockwise_values, jnp.arange(context_block_count, dtype=jnp.int32)))
    return outputs.reshape(CONTEXT_TOKENS, QUERY_HEADS * HEAD_SIZE)
```

```python
import functools

import jax
import jax.numpy as jnp
from jax import lax
from jax.experimental import pallas as pl
from jax.experimental.pallas import tpu as pltpu
from jax.sharding import PartitionSpec as P

MESH = pl.DeviceIdType.MESH
HEAD = 128
HEADS = 4
GROUP = 8
TOKENS = 128
CHIP = 256
WIDE = HEADS * HEAD
SCALE = HEAD**-0.5 * 1.4426950408889634
LOW = -1e30
BF = jnp.bfloat16
F32 = jnp.float32
NT = (((1,), (1,)), ((), ()))
S_SCATTER, S_PLANES, S_FIRST, S_SECOND, S_UP, S_SKIP, S_ROUND, S_RELAY, S_PAIR, S_QUERY, S_OUT, S_COUNT = (
    0, 1, 2, 3, 7, 8, 9, 10, 11, 12, 13, 14)


def dev(x, y, z, c):
    return {"grp": (x // 2) * 4 + y, "sp": (x % 2) * 16 + z * 2 + c}


def kernel(q_hbm, k_hbm, v_hbm, o_hbm, qbuf, obuf, kloc, vloc, kanc, vanc, kfor, vfor, s0, s1, acc, tot, top,
           send, scat_sem, plane_sem, first_sem, second_sem, loc_sem, for_sem, query_sem, own_sem, out_sem, late):
    grp, sp = lax.axis_index("grp"), lax.axis_index("sp")
    x, y = (grp // 4) * 2 + sp // 16, grp % 4
    z, c = (sp // 2) % 8, sp % 2
    j = z % 4
    half = z - j
    low = z < 4
    other = 1 - c
    first_block = jnp.logical_and(x + y == 0, low)

    def remote(src, dst, ssem, rsem, where):
        pltpu.make_async_remote_copy(
            src_ref=src, dst_ref=dst, send_sem=ssem, recv_sem=rsem, device_id=where, device_id_type=MESH
        ).start()

    def wait_kib(sem, kib):
        ref = qbuf if kib == 2048 else kloc.at[pl.ds(0, kib)]
        pltpu.make_async_copy(ref, ref, sem).wait()

    def cols(h):
        return pl.ds(h * HEAD if isinstance(h, int) else pl.multiple_of(h * HEAD, HEAD), HEAD)

    def rows(start, count):
        return pl.ds(pl.multiple_of(start, 16), count)

    barrier = pltpu.get_barrier_semaphore()

    def greet(where):
        pl.semaphore_signal(barrier, 1, device_id=where, device_id_type=MESH)

    greet(dev(x, y, z, other))
    for d in range(1, 4):
        greet(dev((x + d) % 4, y, z, c))
        greet(dev(x, (y + d) % 4, z, c))
        for cc in range(2):
            greet(dev(x, y, half + (j + d) % 4, cc))

    @pl.when(low)
    def _():
        for cc in range(2):
            @pl.when(jnp.logical_or(x + y > 0, c != cc))
            def _():
                greet(dev(0, 0, z, cc))
            for d in range(4):
                greet(dev(x, y, 4 + d, cc))

    pl.semaphore_wait(barrier, 13 + jnp.where(low, jnp.where(first_block, 31, 0), 8))

    def own(ref, h, cc):
        return ref.at[:, pl.ds(cc * WIDE + h * HEAD, HEAD)]

    def send_own(h, zt, kdst, vdst, base, ssem, rsem):
        for cc in range(2):
            for src, dst in ((k_hbm, kdst), (v_hbm, vdst)):
                remote(own(src, h, cc), dst.at[rows(base + c * TOKENS, TOKENS), cols(h)], ssem, rsem, dev(x, y, zt, cc))

    mine = rows(j * CHIP + c * TOKENS, TOKENS)

    def half_of(ref, cc, width):
        return ref.at[:, pl.ds(pl.multiple_of(cc * width, width), width)]

    @pl.when(first_block)
    def _():
        for k in range(8):
            px, py = c * 2 + k // 4, k % 4
            for cc in range(2):
                for src, dst in ((k_hbm, kanc), (v_hbm, vanc)):
                    a = src.at[pl.ds(k * 16, 16), pl.ds(cc * WIDE, WIDE)]
                    b = dst.at[px, py, rows(z * 16, 16), :]
                    if k == 0 and cc == 0:
                        @pl.when(c == 0)
                        def _():
                            pltpu.make_async_copy(a, b, scat_sem).start()

                        @pl.when(c == 1)
                        def _():
                            remote(a, b, send.at[S_SCATTER], scat_sem, dev(px, py, z, cc))
                    else:
                        remote(a, b, send.at[S_SCATTER], scat_sem, dev(px, py, z, cc))

    @pl.when(j < 3)
    def _():
        for h in range(HEADS):
            send_own(h, z + 1, kloc, vloc, j * CHIP, send.at[S_UP], loc_sem.at[j * 4 + h])

    for src, dst in ((k_hbm, kloc), (v_hbm, vloc)):
        pltpu.make_async_copy(half_of(src, c, WIDE), dst.at[mine, :], own_sem).start()
        remote(half_of(src, other, WIDE), dst.at[mine, :], send.at[S_PAIR], own_sem, dev(x, y, z, other))
    for h in range(HEADS):
        wide = GROUP * HEAD
        to = qbuf.at[rows(c * TOKENS, TOKENS), pl.ds(h * wide, wide)]

        def part(cc):
            return q_hbm.at[:, pl.ds(pl.multiple_of(cc * (HEADS * wide) + h * wide, wide), wide)]

        pltpu.make_async_copy(part(c), to, query_sem.at[h]).start()
        remote(part(other), to, send.at[S_QUERY], query_sem.at[h], dev(x, y, z, other))

    @pl.when(jnp.logical_not(low))
    def _():
        def tell(zt, cc):
            pl.semaphore_signal(late, 1, device_id=dev(x, y, zt, cc), device_id_type=MESH)

        tell(7 - z, c)

        @pl.when(z == 7)
        def _():
            tell(1, c)

        @pl.when(z == 5)
        def _():
            tell(0, 0)
            tell(0, 1)

    @pl.when(low)
    def _():
        pl.semaphore_wait(late, jnp.where(z == 0, 3, jnp.where(z == 1, 2, 1)))

    @pl.when(j == 0)
    def _():
        for h in range(HEADS):
            send_own(h, (z + 5) % 8, kfor, vfor, 0, send.at[S_ROUND], for_sem.at[h])
        for h in range(HEADS):
            send_own(h, z + 2, kloc, vloc, 0, send.at[S_SKIP], loc_sem.at[h])

    wait_kib(scat_sem, 32)
    source = jnp.where(low, z, 7 - z)
    for ref in (kanc, vanc):
        piece = ref.at[x, y, rows(source * 16, 16), :]
        for d in range(1, 4):
            remote(piece, piece, send.at[S_PLANES], plane_sem, dev(x, y, half + (j + d) % 4, c))

        @pl.when(low)
        def _():
            remote(piece, piece, send.at[S_PLANES], scat_sem, dev(x, y, 7 - z, c))

    wait_kib(plane_sem, 96)

    for h in range(HEADS):
        for d in range(1, 4):
            a, b = kanc.at[x, y, :, cols(h)], vanc.at[x, y, :, cols(h)]
            remote(a, a, send.at[S_FIRST], first_sem.at[h], dev((x + d) % 4, y, z, c))
            remote(b, b, send.at[S_FIRST], first_sem.at[h], dev(x, (y + d) % 4, z, c))
    for h in range(HEADS):
        wait_kib(first_sem.at[h], 96)
        for d in range(1, 4):
            a, b = kanc.at[:, y, :, cols(h)], vanc.at[x, :, :, cols(h)]
            remote(a, a, send.at[S_SECOND + h], second_sem.at[h], dev(x, (y + d) % 4, z, c))
            remote(b, b, send.at[S_SECOND + h], second_sem.at[h], dev((x + d) % 4, y, z, c))

    def relay(h):
        def hand(kr, vr, krow, srow, zt, sem):
            for a, b in ((kr, kloc), (vr, vloc)):
                remote(
                    a.at[pl.ds(krow, CHIP), cols(h)], b.at[pl.ds(srow, CHIP), cols(h)], send.at[S_RELAY], sem, dev(x, y, zt, c)
                )

        @pl.when(j == 1)
        def _():
            wait_kib(for_sem.at[h], 128)
            hand(kfor, vfor, 0, 0, (z + 6) % 8, loc_sem.at[h])

        @pl.when(j == 2)
        def _():
            wait_kib(loc_sem.at[4 + h], 128)
            hand(kloc, vloc, CHIP, CHIP, z + 1, loc_sem.at[4 + h])

    relay(0)
    wait_kib(own_sem, 512)

    block_zero = jnp.where(first_block, 1e30, 0.0).astype(F32)
    own_rows = rows(j * CHIP, CHIP)

    def with_ones(v):
        return jnp.concatenate([v, jnp.ones_like(v)], axis=1)

    def qcols(h, g):
        return pl.ds(pl.multiple_of(h * (GROUP * HEAD) + g * HEAD, HEAD), HEAD)

    def dot_nt(a, b):
        return lax.dot_general(a, b, NT, preferred_element_type=F32)

    def staged(scores, finish):
        bufs = (s0, s1)
        scores(0, bufs[0])
        for g in range(GROUP):
            if g + 1 < GROUP:
                scores(g + 1, bufs[(g + 1) % 2])
            finish(g, bufs[g % 2])

    def anchor_and_own(h):
        def scores(g, buf):
            q = qbuf[:, qcols(h, g)]
            buf[:, :1024] = dot_nt(q, kanc[:, :, :, cols(h)].reshape(1024, HEAD))
            buf[:, 1024:] = dot_nt(q, kloc[own_rows, cols(h)])

        def finish(g, buf):
            sa, sd = buf[:, :1024], buf[:, 1024:]
            at = lax.broadcasted_iota(jnp.int32, (CHIP, CHIP), 0)
            key = lax.broadcasted_iota(jnp.int32, (CHIP, CHIP), 1)
            sd = jnp.where(at >= key, sd, LOW)
            m = jnp.maximum(jnp.max(sd, 1, keepdims=True), jnp.max(sa, 1, keepdims=True) - block_zero)
            pa = jnp.exp2((sa - (m + block_zero)) * SCALE).astype(BF)
            pd = jnp.exp2((sd - m) * SCALE).astype(BF)
            o = jnp.dot(pa, with_ones(vanc[:, :, :, cols(h)].reshape(1024, HEAD)), preferred_element_type=F32)
            o = o + jnp.dot(pd, with_ones(vloc[own_rows, cols(h)]), preferred_element_type=F32)
            at = qcols(h, g)
            acc[:, at] = o[:, :HEAD]
            tot[:, at] = o[:, HEAD:]
            top[:, at] = jnp.broadcast_to(m, (CHIP, HEAD))
            obuf[:, at] = (o[:, :HEAD] / o[:, HEAD:]).astype(BF)

        staged(scores, finish)

    def earlier(h, count):
        n = count * CHIP

        def scores(g, buf):
            buf[:, :n] = dot_nt(qbuf[:, qcols(h, g)], kloc[:n, cols(h)])

        def finish(g, buf):
            s = buf[:, :n]
            at = qcols(h, g)
            before = top[:, at]
            m = jnp.maximum(before, jnp.broadcast_to(jnp.max(s, 1, keepdims=True), (CHIP, HEAD)))
            p = jnp.exp2((s - jnp.concatenate([m] * (n // HEAD), axis=1)) * SCALE).astype(BF)
            o = jnp.dot(p, with_ones(vloc[:n, cols(h)]), preferred_element_type=F32)
            keep = jnp.exp2((before - m) * SCALE)
            obuf[:, at] = ((acc[:, at] * keep + o[:, :HEAD]) / (tot[:, at] * keep + o[:, HEAD:])).astype(BF)

        staged(scores, finish)

    def deliver(h):
        wide = GROUP * HEAD
        at = pl.ds(pl.multiple_of(h * wide, wide), wide)
        to = o_hbm.at[:, pl.ds(pl.multiple_of(c * (HEADS * wide) + h * wide, wide), wide)]
        remote(obuf.at[rows(other * TOKENS, TOKENS), at], to, send.at[S_OUT], out_sem, dev(x, y, z, other))
        pltpu.make_async_copy(obuf.at[rows(c * TOKENS, TOKENS), at], to, out_sem).start()

    def step(i, _):
        @pl.when(i < HEADS)
        def _():
            wait_kib(query_sem.at[i], 512)
            wait_kib(second_sem.at[i], 384)
            anchor_and_own(i)

            @pl.when(j == 0)
            def _():
                deliver(i)

        @pl.when(i < 2)
        def _():
            relay(i + 1)

        @pl.when(jnp.logical_and(i > 0, j > 0))
        def _():
            h = i - 1
            for count in range(1, 4):
                @pl.when(j == count)
                def _():
                    for slot in range(count):
                        if (count, slot) != (2, 1):
                            wait_kib(loc_sem.at[slot * 4 + h], 128)
                    earlier(h, count)
            deliver(h)

        @pl.when(i == 1)
        def _():
            relay(3)

        return 0

    lax.fori_loop(0, HEADS + 1, step, 0)

    wait_kib(out_sem, 2048)
    wait_kib(send.at[S_OUT], 1024)
    wait_kib(send.at[S_QUERY], 1024)
    wait_kib(send.at[S_PAIR], 256)
    wait_kib(send.at[S_FIRST], 384)
    for h in range(HEADS):
        wait_kib(send.at[S_SECOND + h], 384)

    @pl.when(low)
    def _():
        wait_kib(send.at[S_PLANES], 128)

    @pl.when(jnp.logical_not(low))
    def _():
        wait_kib(send.at[S_PLANES], 96)

    @pl.when(jnp.logical_and(first_block, c == 0))
    def _():
        wait_kib(send.at[S_SCATTER], 480)

    @pl.when(jnp.logical_and(first_block, c == 1))
    def _():
        wait_kib(send.at[S_SCATTER], 512)

    @pl.when(j < 3)
    def _():
        wait_kib(send.at[S_UP], 512)

    @pl.when(j == 0)
    def _():
        wait_kib(send.at[S_SKIP], 512)
        wait_kib(send.at[S_ROUND], 512)

    @pl.when(jnp.logical_or(j == 1, j == 2))
    def _():
        wait_kib(send.at[S_RELAY], 512)


def attend(queries, keys, values):
    dma = pltpu.SemaphoreType.DMA
    wide = HEADS * GROUP * HEAD
    return pl.pallas_call(
        kernel,
        out_shape=jax.ShapeDtypeStruct(queries.shape, BF),
        in_specs=[pl.BlockSpec(memory_space=pl.ANY)] * 3,
        out_specs=pl.BlockSpec(memory_space=pl.ANY),
        scratch_shapes=[
            pltpu.VMEM((CHIP, wide), BF),
            pltpu.VMEM((CHIP, wide), BF),
            pltpu.VMEM((1024, WIDE), BF),
            pltpu.VMEM((1024, WIDE), BF),
            pltpu.VMEM((4, 4, 64, WIDE), BF),
            pltpu.VMEM((4, 4, 64, WIDE), BF),
            pltpu.VMEM((CHIP, WIDE), BF),
            pltpu.VMEM((CHIP, WIDE), BF),
            pltpu.VMEM((CHIP, 1280), F32),
            pltpu.VMEM((CHIP, 1280), F32),
            pltpu.VMEM((CHIP, wide), F32),
            pltpu.VMEM((CHIP, wide), F32),
            pltpu.VMEM((CHIP, wide), F32),
            dma((S_COUNT,)),
            dma(()),
            dma(()),
            dma((4,)),
            dma((4,)),
            dma((12,)),
            dma((4,)),
            dma((4,)),
            dma(()),
            dma(()),
            pltpu.SemaphoreType.REGULAR,
        ],
        compiler_params=pltpu.CompilerParams(collective_id=0, has_side_effects=True, vmem_limit_bytes=56 << 20),
    )(queries, keys, values)


def solution(mesh):
    return jax.shard_map(
        attend,
        mesh=mesh,
        in_specs=(P(("grp", "sp"), None),) * 3,
        out_specs=P(("grp", "sp"), None),
        check_vma=False,
    )
```

```python
import functools

import jax
import jax.numpy as jnp
from jax import lax
from jax.experimental import pallas as pl
from jax.experimental.pallas import tpu as pltpu
from jax.sharding import PartitionSpec as P

MESH = pl.DeviceIdType.MESH
HEAD = 128
HEADS = 4
GROUP = 8
TOKENS = 128
CHIP = 256
WIDE = HEADS * HEAD
SCALE = HEAD**-0.5 * 1.4426950408889634
LOW = -1e30
ROUND_LOW, ROUND_HIGH = (2, 3), (0, 1, 2, 3)
PARTS = ((0, 2 * HEAD), (2 * HEAD, 2 * HEAD))
BF = jnp.bfloat16
F32 = jnp.float32
NT = (((1,), (1,)), ((), ()))
S_SCATTER, S_PLANES, S_FIRST, S_SECOND, S_UP, S_SKIP, S_ROUND, S_RELAY, S_PAIR, S_QUERY, S_OUT, S_COUNT = (
    0, 1, 2, 3, 7, 8, 9, 10, 11, 12, 13, 14)


def dev(x, y, z, c):
    return {"grp": (x // 2) * 4 + y, "sp": (x % 2) * 16 + z * 2 + c}


def kernel(q_hbm, k_hbm, v_hbm, o_hbm, qbuf, obuf, kloc, vloc, kanc, vanc, kfor, vfor, s0, s1, acc, tot, top,
           send, scat_sem, plane_sem, first_sem, second_sem, loc_sem, for_sem, query_sem, own_sem, out_sem, late):
    grp, sp = lax.axis_index("grp"), lax.axis_index("sp")
    x, y = (grp // 4) * 2 + sp // 16, grp % 4
    z, c = (sp // 2) % 8, sp % 2
    j = z % 4
    half = z - j
    low = z < 4
    other = 1 - c
    first_block = jnp.logical_and(x + y == 0, low)

    def remote(src, dst, ssem, rsem, where):
        pltpu.make_async_remote_copy(
            src_ref=src, dst_ref=dst, send_sem=send.at[ssem], recv_sem=rsem, device_id=where, device_id_type=MESH
        ).start()

    def wait_kib(sem, kib):
        ref = qbuf if kib == 2048 else kloc.at[pl.ds(0, kib)]
        pltpu.make_async_copy(ref, ref, sem).wait()

    def wait_sent(index, kib):
        wait_kib(send.at[index], kib)

    def cols(h):
        return pl.ds(h * HEAD if isinstance(h, int) else pl.multiple_of(h * HEAD, HEAD), HEAD)

    def rows(start, count):
        return pl.ds(pl.multiple_of(start, 16), count)

    barrier = pltpu.get_barrier_semaphore()

    def greet(where):
        pl.semaphore_signal(barrier, 1, device_id=where, device_id_type=MESH)

    greet(dev(x, y, z, other))
    for d in range(1, 4):
        greet(dev((x + d) % 4, y, z, c))
        greet(dev(x, (y + d) % 4, z, c))
        for cc in range(2):
            greet(dev(x, y, half + (j + d) % 4, cc))

    @pl.when(low)
    def _():
        for cc in range(2):
            @pl.when(jnp.logical_or(x + y > 0, c != cc))
            def _():
                greet(dev(0, 0, z, cc))
            for d in range(4):
                greet(dev(x, y, 4 + d, cc))

    pl.semaphore_wait(barrier, 13 + jnp.where(low, jnp.where(first_block, 31, 0), 8))

    @pl.when(jnp.logical_not(low))
    def _():
        def tell(zt, cc):
            pl.semaphore_signal(late, 1, device_id=dev(x, y, zt, cc), device_id_type=MESH)

        tell(7 - z, c)

        @pl.when(z == 7)
        def _():
            tell(1, c)

        @pl.when(z == 5)
        def _():
            tell(0, 0)
            tell(0, 1)

    @pl.when(first_block)
    def _():
        for part in range(2):
            for k in range(8):
                px, py = c * 2 + k // 4, k % 4
                for cc in range(2):
                    for src, dst in ((k_hbm, kanc), (v_hbm, vanc)):
                        lo, wide = PARTS[part]
                        a = src.at[pl.ds(k * 16, 16), pl.ds(cc * WIDE + lo, wide)]
                        b = dst.at[px, py, rows(z * 16, 16), pl.ds(lo, wide)]
                        if k == 0 and cc == 0:
                            @pl.when(c == 0)
                            def _():
                                pltpu.make_async_copy(a, b, scat_sem.at[part]).start()

                            @pl.when(c == 1)
                            def _():
                                remote(a, b, S_SCATTER, scat_sem.at[part], dev(px, py, z, cc))
                        else:
                            remote(a, b, S_SCATTER, scat_sem.at[part], dev(px, py, z, cc))

    def own(ref, h, cc):
        return ref.at[:, pl.ds(cc * WIDE + h * HEAD, HEAD)]

    def send_own(h, zt, kdst, vdst, base, ssem, rsem):
        for cc in range(2):
            for src, dst in ((k_hbm, kdst), (v_hbm, vdst)):
                remote(own(src, h, cc), dst.at[rows(base + c * TOKENS, TOKENS), cols(h)], ssem, rsem, dev(x, y, zt, cc))

    def up(heads):
        @pl.when(j < 3)
        def _():
            for h in heads:
                send_own(h, z + 1, kloc, vloc, j * CHIP, S_UP, loc_sem.at[j * 4 + h])

    def round_ring(heads):
        for h in heads:
            send_own(h, (z + 5) % 8, kfor, vfor, 0, S_ROUND, for_sem.at[h])

    mine = rows(j * CHIP + c * TOKENS, TOKENS)

    def half_of(ref, cc, width):
        return ref.at[:, pl.ds(pl.multiple_of(cc * width, width), width)]

    up((0, 1))
    for src, dst in ((k_hbm, kloc), (v_hbm, vloc)):
        pltpu.make_async_copy(half_of(src, c, WIDE), dst.at[mine, :], own_sem).start()
        remote(half_of(src, other, WIDE), dst.at[mine, :], S_PAIR, own_sem, dev(x, y, z, other))

    source = jnp.where(low, z, 7 - z)

    def pieces(part):
        lo, wide = PARTS[part]
        return [ref.at[x, y, rows(source * 16, 16), pl.ds(lo, wide)] for ref in (kanc, vanc)]

    def to_half(part):
        wait_kib(scat_sem.at[part], PARTS[part][1] // 16)
        for piece in pieces(part):
            for d in range(1, 4):
                remote(piece, piece, S_PLANES, plane_sem.at[part], dev(x, y, half + (j + d) % 4, c))

    def to_later(part):
        @pl.when(low)
        def _():
            for piece in pieces(part):
                remote(piece, piece, S_PLANES, scat_sem.at[part], dev(x, y, 7 - z, c))

    for h in range(HEADS):
        wide = GROUP * HEAD
        to = qbuf.at[rows(c * TOKENS, TOKENS), pl.ds(h * wide, wide)]

        def part_of(cc):
            return q_hbm.at[:, pl.ds(pl.multiple_of(cc * (HEADS * wide) + h * wide, wide), wide)]

        pltpu.make_async_copy(part_of(c), to, query_sem.at[h]).start()
        remote(part_of(other), to, S_QUERY, query_sem.at[h], dev(x, y, z, other))

    def hand(h, kr, vr, krow, srow, zt, sem):
        for a, b in ((kr, kloc), (vr, vloc)):
            remote(
                a.at[pl.ds(krow, CHIP), cols(h)], b.at[pl.ds(srow, CHIP), cols(h)], S_RELAY, sem, dev(x, y, zt, c)
            )

    def relay_next(h):
        wait_kib(loc_sem.at[4 + h], 128)
        hand(h, kloc, vloc, CHIP, CHIP, z + 1, loc_sem.at[4 + h])

    def relay(h):
        for at, heads in ((5, ROUND_LOW), (1, ROUND_HIGH)):
            if h in heads:
                @pl.when(z == at)
                def _():
                    wait_kib(for_sem.at[h], 128)
                    hand(h, kfor, vfor, 0, 0, (z + 6) % 8, loc_sem.at[h])

        for at, heads in ((2, ROUND_LOW), (6, ROUND_HIGH)):
            if h not in heads:
                @pl.when(z == at)
                def _():
                    wait_kib(loc_sem.at[h], 128)
                    hand(h, kloc, vloc, 0, 0, z + 1, loc_sem.at[h])

    block_zero = jnp.where(first_block, 1e30, 0.0).astype(F32)
    own_rows = rows(j * CHIP, CHIP)

    def with_ones(v):
        return jnp.concatenate([v, jnp.ones_like(v)], axis=1)

    def qcols(h, g):
        return pl.ds(pl.multiple_of(h * (GROUP * HEAD) + g * HEAD, HEAD), HEAD)

    def dot_nt(a, b):
        return lax.dot_general(a, b, NT, preferred_element_type=F32)

    def staged(scores, finish):
        bufs = (s0, s1)
        scores(0, bufs[0])
        for g in range(GROUP):
            if g + 1 < GROUP:
                scores(g + 1, bufs[(g + 1) % 2])
            finish(g, bufs[g % 2])

    def near(h, n):
        where = rows((j + 1) * CHIP - n, n)

        def scores(g, buf):
            buf[:, :n] = dot_nt(qbuf[:, qcols(h, g)], kloc[where, cols(h)])

        def finish(g, buf):
            at = lax.broadcasted_iota(jnp.int32, (CHIP, CHIP), 0)
            key = lax.broadcasted_iota(jnp.int32, (CHIP, CHIP), 1)
            s = jnp.where(at >= key, buf[:, n - CHIP : n], LOW)
            if n > CHIP:
                s = jnp.concatenate([buf[:, : n - CHIP], s], axis=1)
            weigh(h, g, s, vloc[where, cols(h)], 0.0, True, False)

        staged(scores, finish)

    def far(h, n):
        def scores(g, buf):
            buf[:, :n] = dot_nt(qbuf[:, qcols(h, g)], kloc[:n, cols(h)])

        def finish(g, buf):
            weigh(h, g, buf[:, :n], vloc[:n, cols(h)], 0.0, False, True)

        staged(scores, finish)

    def anchor(h, last):
        n = 1024

        def scores(g, buf):
            buf[...] = dot_nt(qbuf[:, qcols(h, g)], kanc[:, :, :, cols(h)].reshape(n, HEAD))

        def finish(g, buf):
            weigh(h, g, buf[...], vanc[:, :, :, cols(h)].reshape(n, HEAD), block_zero, False, last)

        staged(scores, finish)

    def weigh(h, g, s, v, away, first, last):
        at = qcols(h, g)
        m = jnp.broadcast_to(jnp.max(s, 1, keepdims=True), (CHIP, HEAD)) - away
        if not first:
            before = top[:, at]
            m = jnp.maximum(before, m)
        p = jnp.exp2((s - jnp.concatenate([m + away] * (s.shape[1] // HEAD), axis=1)) * SCALE).astype(BF)
        o = jnp.dot(p, with_ones(v), preferred_element_type=F32)
        weighted, total = o[:, :HEAD], o[:, HEAD:]
        if not first:
            keep = jnp.exp2((before - m) * SCALE)
            weighted, total = acc[:, at] * keep + weighted, tot[:, at] * keep + total
        if last:
            obuf[:, at] = (weighted / total).astype(BF)
        else:
            acc[:, at] = weighted
            tot[:, at] = total
            top[:, at] = m

    def early(h):
        wait_kib(query_sem.at[h], 512)

        @pl.when(j == 0)
        def _():
            near(h, CHIP)

        @pl.when(j > 0)
        def _():
            @pl.when(j != 2)
            def _():
                wait_kib(loc_sem.at[(j - 1) * 4 + h], 128)

            @pl.when(j == 2)
            def _():
                relay_next(h)

            near(h, 2 * CHIP)

    def late_part(h):
        @pl.when(j == 2)
        def _():
            handed = functools.reduce(
                jnp.logical_or,
                [
                    jnp.logical_and(z == at, h == hh)
                    for at, heads in ((2, ROUND_LOW), (6, ROUND_HIGH))
                    for hh in range(HEADS)
                    if hh not in heads
                ],
                False,
            )

            @pl.when(jnp.logical_not(handed))
            def _():
                wait_kib(loc_sem.at[h], 128)

            far(h, CHIP)

        @pl.when(j == 3)
        def _():
            wait_kib(loc_sem.at[h], 128)
            wait_kib(loc_sem.at[4 + h], 128)
            far(h, 2 * CHIP)

    def deliver(h):
        wide = GROUP * HEAD
        at = pl.ds(pl.multiple_of(h * wide, wide), wide)
        to = o_hbm.at[:, pl.ds(pl.multiple_of(c * (HEADS * wide) + h * wide, wide), wide)]
        remote(obuf.at[rows(other * TOKENS, TOKENS), at], to, S_OUT, out_sem, dev(x, y, z, other))
        pltpu.make_async_copy(obuf.at[rows(c * TOKENS, TOKENS), at], to, out_sem).start()

    def first(h):
        for d in range(1, 4):
            a, b = kanc.at[x, y, :, cols(h)], vanc.at[x, y, :, cols(h)]
            remote(a, a, S_FIRST, first_sem.at[h], dev((x + d) % 4, y, z, c))
            remote(b, b, S_FIRST, first_sem.at[h], dev(x, (y + d) % 4, z, c))

    def second(h):
        wait_kib(first_sem.at[h], 96)
        for d in range(1, 4):
            a, b = kanc.at[:, y, :, cols(h)], vanc.at[x, :, :, cols(h)]
            remote(a, a, S_SECOND + h, second_sem.at[h], dev(x, (y + d) % 4, z, c))
            remote(b, b, S_SECOND + h, second_sem.at[h], dev((x + d) % 4, y, z, c))

    wait_kib(own_sem, 512)
    pl.when(jnp.logical_not(low))(lambda: early(0))
    to_half(0)

    @pl.when(low)
    def _():
        pl.semaphore_wait(late, jnp.where(z == 0, 3, jnp.where(z == 1, 2, 1)))

    to_later(0)
    wait_kib(plane_sem.at[0], 48)
    first(0)
    first(1)
    to_half(1)
    pl.when(z == 4)(lambda: round_ring(ROUND_HIGH))
    to_later(1)
    up((2, 3))

    @pl.when(j == 0)
    def _():
        for h in range(HEADS):
            send_own(h, z + 2, kloc, vloc, 0, S_SKIP, loc_sem.at[h])

    pl.when(low)(lambda: early(0))
    second(0)
    second(1)
    early(1)
    wait_kib(plane_sem.at[1], 48)
    first(2)
    first(3)
    pl.when(z == 0)(lambda: round_ring(ROUND_LOW))
    relay(0)
    second(2)
    second(3)
    early(2)
    early(3)
    relay(1)
    relay(2)

    def step(h, _):
        wait_kib(second_sem.at[h], 384)

        @pl.when(j < 2)
        def _():
            anchor(h, True)

        @pl.when(j > 1)
        def _():
            anchor(h, False)

        @pl.when(h == 0)
        def _():
            relay(3)

        late_part(h)
        deliver(h)
        return 0

    lax.fori_loop(0, HEADS, step, 0)

    wait_kib(out_sem, 2048)
    wait_sent(S_OUT, 1024)
    wait_sent(S_QUERY, 1024)
    wait_sent(S_PAIR, 256)
    wait_sent(S_FIRST, 384)
    for h in range(HEADS):
        wait_sent(S_SECOND + h, 384)

    @pl.when(low)
    def _():
        wait_sent(S_PLANES, 128)

    @pl.when(jnp.logical_not(low))
    def _():
        wait_sent(S_PLANES, 96)

    @pl.when(jnp.logical_and(first_block, c == 0))
    def _():
        wait_sent(S_SCATTER, 480)

    @pl.when(jnp.logical_and(first_block, c == 1))
    def _():
        wait_sent(S_SCATTER, 512)

    @pl.when(j < 3)
    def _():
        wait_sent(S_UP, 512)

    @pl.when(j == 0)
    def _():
        wait_sent(S_SKIP, 512)

    for base, near, far in ((0, ROUND_LOW, ROUND_HIGH), (4, ROUND_HIGH, ROUND_LOW)):
        for at, index, count in (
            (0, S_ROUND, len(near)),
            (1, S_RELAY, len(far)),
            (2, S_RELAY, 2 * HEADS - len(near)),
        ):
            if count:
                @pl.when(z == base + at)
                def _():
                    wait_sent(index, 128 * count)


def place(src, dst, buf, sems):
    reads = [pltpu.make_async_copy(src.at[pl.ds(16 * i, 16)], buf.at[pl.ds(16 * i, 16)], sems.at[i]) for i in range(8)]
    writes = [pltpu.make_async_copy(buf.at[pl.ds(16 * i, 16)], dst.at[pl.ds(16 * i, 16)], sems.at[8 + i]) for i in range(8)]
    for copy in reads:
        copy.start()
    for read, write in zip(reads, writes):
        read.wait()
        write.start()
    for copy in writes:
        copy.wait()


def attend(queries, keys, values):
    dma = pltpu.SemaphoreType.DMA
    wide = HEADS * GROUP * HEAD
    result = pl.pallas_call(
        kernel,
        out_shape=jax.ShapeDtypeStruct(queries.shape, BF),
        in_specs=[pl.BlockSpec(memory_space=pl.ANY)] * 3,
        out_specs=pl.BlockSpec(memory_space=pl.ANY),
        scratch_shapes=[
            pltpu.VMEM((CHIP, wide), BF),
            pltpu.VMEM((CHIP, wide), BF),
            pltpu.VMEM((1024, WIDE), BF),
            pltpu.VMEM((1024, WIDE), BF),
            pltpu.VMEM((4, 4, 64, WIDE), BF),
            pltpu.VMEM((4, 4, 64, WIDE), BF),
            pltpu.VMEM((CHIP, WIDE), BF),
            pltpu.VMEM((CHIP, WIDE), BF),
            pltpu.VMEM((CHIP, 1024), F32),
            pltpu.VMEM((CHIP, 1024), F32),
            pltpu.VMEM((CHIP, wide), F32),
            pltpu.VMEM((CHIP, wide), F32),
            pltpu.VMEM((CHIP, wide), F32),
            dma((S_COUNT,)),
            dma((2,)),
            dma((2,)),
            dma((4,)),
            dma((4,)),
            dma((12,)),
            dma((4,)),
            dma((4,)),
            dma(()),
            dma(()),
            pltpu.SemaphoreType.REGULAR,
        ],
        compiler_params=pltpu.CompilerParams(collective_id=0, has_side_effects=True, vmem_limit_bytes=56 << 20),
    )(queries, keys, values)
    return pl.pallas_call(
        place,
        out_shape=jax.ShapeDtypeStruct(queries.shape, BF),
        in_specs=[pl.BlockSpec(memory_space=pl.ANY)],
        out_specs=pl.BlockSpec(memory_space=pl.ANY),
        scratch_shapes=[pltpu.VMEM((128, 8192), BF), pltpu.SemaphoreType.DMA((16,))],
    )(result)


def solution(mesh):
    return jax.shard_map(
        attend,
        mesh=mesh,
        in_specs=(P(("grp", "sp"), None),) * 3,
        out_specs=P(("grp", "sp"), None),
        check_vma=False,
    )
```

```python
import functools

import jax
import jax.numpy as jnp
from jax import lax
from jax.experimental import pallas as pl
from jax.experimental.pallas import tpu as pltpu
from jax.sharding import PartitionSpec as P

MESH = pl.DeviceIdType.MESH
HEAD = 128
HEADS = 4
GROUP = 8
TOKENS = 128
CHIP = 256
WIDE = HEADS * HEAD
SCALE = HEAD**-0.5 * 1.4426950408889634
LOW = -1e30
ROUND_LOW, ROUND_HIGH = (2, 3), (0, 1, 2, 3)
PARTS = ((0, 2 * HEAD), (2 * HEAD, 2 * HEAD))
BF = jnp.bfloat16
F32 = jnp.float32
NT = (((1,), (1,)), ((), ()))
S_SCATTER, S_PLANES, S_FIRST, S_SECOND, S_UP, S_SKIP, S_ROUND, S_RELAY, S_PAIR, S_QUERY, S_OUT, S_COUNT = (
    0, 1, 2, 3, 7, 8, 9, 10, 11, 12, 13, 14)


def dev(x, y, z, c):
    return {"grp": (x // 2) * 4 + y, "sp": (x % 2) * 16 + z * 2 + c}


def kernel(q_hbm, k_hbm, v_hbm, o_hbm, qbuf, obuf, kloc, vloc, kanc, vanc, kfor, vfor, s0, s1, acc, tot, top,
           send, scat_sem, plane_sem, first_sem, second_sem, loc_sem, for_sem, query_sem, own_sem, out_sem, late):
    grp, sp = lax.axis_index("grp"), lax.axis_index("sp")
    x, y = (grp // 4) * 2 + sp // 16, grp % 4
    z, c = (sp // 2) % 8, sp % 2
    j = z % 4
    half = z - j
    low = z < 4
    other = 1 - c
    first_block = jnp.logical_and(x + y == 0, low)

    def remote(src, dst, ssem, rsem, where):
        pltpu.make_async_remote_copy(
            src_ref=src, dst_ref=dst, send_sem=send.at[ssem], recv_sem=rsem, device_id=where, device_id_type=MESH
        ).start()

    def wait_kib(sem, kib):
        ref = qbuf if kib == 2048 else kloc.at[pl.ds(0, kib)]
        pltpu.make_async_copy(ref, ref, sem).wait()

    def wait_sent(index, kib):
        wait_kib(send.at[index], kib)

    def cols(h):
        return pl.ds(h * HEAD if isinstance(h, int) else pl.multiple_of(h * HEAD, HEAD), HEAD)

    def rows(start, count):
        return pl.ds(pl.multiple_of(start, 16), count)

    barrier = pltpu.get_barrier_semaphore()

    def greet(where):
        pl.semaphore_signal(barrier, 1, device_id=where, device_id_type=MESH)

    greet(dev(x, y, z, other))
    for d in range(1, 4):
        greet(dev((x + d) % 4, y, z, c))
        greet(dev(x, (y + d) % 4, z, c))
        for cc in range(2):
            greet(dev(x, y, half + (j + d) % 4, cc))

    @pl.when(low)
    def _():
        for cc in range(2):
            @pl.when(jnp.logical_or(x + y > 0, c != cc))
            def _():
                greet(dev(0, 0, z, cc))
            for d in range(4):
                greet(dev(x, y, 4 + d, cc))

    pl.semaphore_wait(barrier, 13 + jnp.where(low, jnp.where(first_block, 31, 0), 8))

    @pl.when(jnp.logical_not(low))
    def _():
        def tell(zt, cc):
            pl.semaphore_signal(late, 1, device_id=dev(x, y, zt, cc), device_id_type=MESH)

        tell(7 - z, c)

        @pl.when(z == 7)
        def _():
            tell(1, c)

        @pl.when(z == 5)
        def _():
            tell(0, 0)
            tell(0, 1)

    @pl.when(first_block)
    def _():
        for part in range(2):
            for k in range(8):
                px, py = c * 2 + k // 4, k % 4
                for cc in range(2):
                    for src, dst in ((k_hbm, kanc), (v_hbm, vanc)):
                        lo, wide = PARTS[part]
                        a = src.at[pl.ds(k * 16, 16), pl.ds(cc * WIDE + lo, wide)]
                        b = dst.at[px, py, rows(z * 16, 16), pl.ds(lo, wide)]
                        if k == 0 and cc == 0:
                            @pl.when(c == 0)
                            def _():
                                pltpu.make_async_copy(a, b, scat_sem.at[part]).start()

                            @pl.when(c == 1)
                            def _():
                                remote(a, b, S_SCATTER, scat_sem.at[part], dev(px, py, z, cc))
                        else:
                            remote(a, b, S_SCATTER, scat_sem.at[part], dev(px, py, z, cc))

    def own(ref, h, cc):
        return ref.at[:, pl.ds(cc * WIDE + h * HEAD, HEAD)]

    def send_own(h, zt, kdst, vdst, base, ssem, rsem):
        for cc in range(2):
            for src, dst in ((k_hbm, kdst), (v_hbm, vdst)):
                remote(own(src, h, cc), dst.at[rows(base + c * TOKENS, TOKENS), cols(h)], ssem, rsem, dev(x, y, zt, cc))

    def up(heads):
        @pl.when(j < 3)
        def _():
            for h in heads:
                send_own(h, z + 1, kloc, vloc, j * CHIP, S_UP, loc_sem.at[j * 4 + h])

    def round_ring(heads):
        for h in heads:
            send_own(h, (z + 5) % 8, kfor, vfor, 0, S_ROUND, for_sem.at[h])

    mine = rows(j * CHIP + c * TOKENS, TOKENS)

    def half_of(ref, cc, width):
        return ref.at[:, pl.ds(pl.multiple_of(cc * width, width), width)]

    up((0, 1))
    for src, dst in ((k_hbm, kloc), (v_hbm, vloc)):
        pltpu.make_async_copy(half_of(src, c, WIDE), dst.at[mine, :], own_sem).start()
        remote(half_of(src, other, WIDE), dst.at[mine, :], S_PAIR, own_sem, dev(x, y, z, other))

    source = jnp.where(low, z, 7 - z)

    def pieces(part):
        lo, wide = PARTS[part]
        return [ref.at[x, y, rows(source * 16, 16), pl.ds(lo, wide)] for ref in (kanc, vanc)]

    def to_half(part):
        wait_kib(scat_sem.at[part], PARTS[part][1] // 16)
        for piece in pieces(part):
            for d in range(1, 4):
                remote(piece, piece, S_PLANES, plane_sem.at[part], dev(x, y, half + (j + d) % 4, c))

    def to_later(part):
        @pl.when(low)
        def _():
            for piece in pieces(part):
                remote(piece, piece, S_PLANES, scat_sem.at[part], dev(x, y, 7 - z, c))

    for h in range(HEADS):
        wide = GROUP * HEAD
        to = qbuf.at[rows(c * TOKENS, TOKENS), pl.ds(h * wide, wide)]

        def part_of(cc):
            return q_hbm.at[:, pl.ds(pl.multiple_of(cc * (HEADS * wide) + h * wide, wide), wide)]

        pltpu.make_async_copy(part_of(c), to, query_sem.at[h]).start()
        remote(part_of(other), to, S_QUERY, query_sem.at[h], dev(x, y, z, other))

    def hand(h, kr, vr, krow, srow, zt, sem):
        for a, b in ((kr, kloc), (vr, vloc)):
            remote(
                a.at[pl.ds(krow, CHIP), cols(h)], b.at[pl.ds(srow, CHIP), cols(h)], S_RELAY, sem, dev(x, y, zt, c)
            )

    def relay_next(h):
        wait_kib(loc_sem.at[4 + h], 128)
        hand(h, kloc, vloc, CHIP, CHIP, z + 1, loc_sem.at[4 + h])

    def relay(h):
        for at, heads in ((5, ROUND_LOW), (1, ROUND_HIGH)):
            if h in heads:
                @pl.when(z == at)
                def _():
                    wait_kib(for_sem.at[h], 128)
                    hand(h, kfor, vfor, 0, 0, (z + 6) % 8, loc_sem.at[h])

        for at, heads in ((2, ROUND_LOW), (6, ROUND_HIGH)):
            if h not in heads:
                @pl.when(z == at)
                def _():
                    wait_kib(loc_sem.at[h], 128)
                    hand(h, kloc, vloc, 0, 0, z + 1, loc_sem.at[h])

    block_zero = jnp.where(first_block, 1e30, 0.0).astype(F32)
    own_rows = rows(j * CHIP, CHIP)

    def with_ones(v):
        return jnp.concatenate([v, jnp.ones_like(v)], axis=1)

    def qcols(h, g):
        return pl.ds(pl.multiple_of(h * (GROUP * HEAD) + g * HEAD, HEAD), HEAD)

    def dot_nt(a, b):
        return lax.dot_general(a, b, NT, preferred_element_type=F32)

    def staged(scores, finish):
        bufs = (s0, s1)
        scores(0, bufs[0])
        for g in range(GROUP):
            if g + 1 < GROUP:
                scores(g + 1, bufs[(g + 1) % 2])
            finish(g, bufs[g % 2])

    def near(h, n):
        where = rows((j + 1) * CHIP - n, n)

        def scores(g, buf):
            buf[:, :n] = dot_nt(qbuf[:, qcols(h, g)], kloc[where, cols(h)])

        def finish(g, buf):
            at = lax.broadcasted_iota(jnp.int32, (CHIP, CHIP), 0)
            key = lax.broadcasted_iota(jnp.int32, (CHIP, CHIP), 1)
            s = jnp.where(at >= key, buf[:, n - CHIP : n], LOW)
            if n > CHIP:
                s = jnp.concatenate([buf[:, : n - CHIP], s], axis=1)
            weigh(h, g, s, vloc[where, cols(h)], 0.0, True, False)

        staged(scores, finish)

    def far(h, n):
        def scores(g, buf):
            buf[:, :n] = dot_nt(qbuf[:, qcols(h, g)], kloc[:n, cols(h)])

        def finish(g, buf):
            weigh(h, g, buf[:, :n], vloc[:n, cols(h)], 0.0, False, True)

        staged(scores, finish)

    def anchor(h, last):
        n = 1024

        def scores(g, buf):
            buf[...] = dot_nt(qbuf[:, qcols(h, g)], kanc[:, :, :, cols(h)].reshape(n, HEAD))

        def finish(g, buf):
            weigh(h, g, buf[...], vanc[:, :, :, cols(h)].reshape(n, HEAD), block_zero, False, last)

        staged(scores, finish)

    def weigh(h, g, s, v, away, first, last):
        at = qcols(h, g)
        m = jnp.broadcast_to(jnp.max(s, 1, keepdims=True), (CHIP, HEAD)) - away
        if not first:
            before = top[:, at]
            m = jnp.maximum(before, m)
        p = jnp.exp2((s - jnp.concatenate([m + away] * (s.shape[1] // HEAD), axis=1)) * SCALE).astype(BF)
        o = jnp.dot(p, with_ones(v), preferred_element_type=F32)
        weighted, total = o[:, :HEAD], o[:, HEAD:]
        if not first:
            keep = jnp.exp2((before - m) * SCALE)
            weighted, total = acc[:, at] * keep + weighted, tot[:, at] * keep + total
        if last:
            obuf[:, at] = (weighted / total).astype(BF)
        else:
            acc[:, at] = weighted
            tot[:, at] = total
            top[:, at] = m

    def early(h):
        wait_kib(query_sem.at[h], 512)

        @pl.when(j == 0)
        def _():
            near(h, CHIP)

        @pl.when(j > 0)
        def _():
            @pl.when(j != 2)
            def _():
                wait_kib(loc_sem.at[(j - 1) * 4 + h], 128)

            @pl.when(j == 2)
            def _():
                relay_next(h)

            near(h, 2 * CHIP)

    def late_part(h):
        @pl.when(j == 2)
        def _():
            handed = functools.reduce(
                jnp.logical_or,
                [
                    jnp.logical_and(z == at, h == hh)
                    for at, heads in ((2, ROUND_LOW), (6, ROUND_HIGH))
                    for hh in range(HEADS)
                    if hh not in heads
                ],
                False,
            )

            @pl.when(jnp.logical_not(handed))
            def _():
                wait_kib(loc_sem.at[h], 128)

            far(h, CHIP)

        @pl.when(j == 3)
        def _():
            wait_kib(loc_sem.at[h], 128)
            wait_kib(loc_sem.at[4 + h], 128)
            far(h, 2 * CHIP)

    def anchor_part(h):
        wait_kib(second_sem.at[h], 384)

        @pl.when(j < 2)
        def _():
            anchor(h, True)

        @pl.when(j > 1)
        def _():
            anchor(h, False)

    def deliver(h):
        wide = GROUP * HEAD
        at = pl.ds(pl.multiple_of(h * wide, wide), wide)
        to = o_hbm.at[:, pl.ds(pl.multiple_of(c * (HEADS * wide) + h * wide, wide), wide)]
        remote(obuf.at[rows(other * TOKENS, TOKENS), at], to, S_OUT, out_sem, dev(x, y, z, other))
        pltpu.make_async_copy(obuf.at[rows(c * TOKENS, TOKENS), at], to, out_sem).start()

    def first(h):
        for d in range(1, 4):
            a, b = kanc.at[x, y, :, cols(h)], vanc.at[x, y, :, cols(h)]
            remote(a, a, S_FIRST, first_sem.at[h], dev((x + d) % 4, y, z, c))
            remote(b, b, S_FIRST, first_sem.at[h], dev(x, (y + d) % 4, z, c))

    def second(h):
        wait_kib(first_sem.at[h], 96)
        for d in range(1, 4):
            a, b = kanc.at[:, y, :, cols(h)], vanc.at[x, :, :, cols(h)]
            remote(a, a, S_SECOND + h, second_sem.at[h], dev(x, (y + d) % 4, z, c))
            remote(b, b, S_SECOND + h, second_sem.at[h], dev((x + d) % 4, y, z, c))

    wait_kib(own_sem, 512)
    pl.when(jnp.logical_not(low))(lambda: early(0))
    to_half(0)

    @pl.when(low)
    def _():
        pl.semaphore_wait(late, jnp.where(z == 0, 3, jnp.where(z == 1, 2, 1)))

    to_later(0)
    wait_kib(plane_sem.at[0], 48)
    first(0)
    first(1)
    to_half(1)
    pl.when(z == 4)(lambda: round_ring(ROUND_HIGH))
    to_later(1)
    up((2, 3))

    @pl.when(j == 0)
    def _():
        for h in range(HEADS):
            send_own(h, z + 2, kloc, vloc, 0, S_SKIP, loc_sem.at[h])

    pl.when(low)(lambda: early(0))
    second(0)
    second(1)
    early(1)
    wait_kib(plane_sem.at[1], 48)
    first(2)
    first(3)
    pl.when(z == 0)(lambda: round_ring(ROUND_LOW))
    relay(0)
    anchor_part(0)
    second(2)
    early(2)
    second(3)
    relay(1)
    early(3)
    relay(2)

    def step(h, _):
        pl.when(h > 0)(lambda: anchor_part(h))

        @pl.when(h == 0)
        def _():
            relay(3)

        late_part(h)
        deliver(h)
        return 0

    lax.fori_loop(0, HEADS, step, 0)

    wait_kib(out_sem, 2048)
    wait_sent(S_OUT, 1024)
    wait_sent(S_QUERY, 1024)
    wait_sent(S_PAIR, 256)
    wait_sent(S_FIRST, 384)
    for h in range(HEADS):
        wait_sent(S_SECOND + h, 384)

    @pl.when(low)
    def _():
        wait_sent(S_PLANES, 128)

    @pl.when(jnp.logical_not(low))
    def _():
        wait_sent(S_PLANES, 96)

    @pl.when(jnp.logical_and(first_block, c == 0))
    def _():
        wait_sent(S_SCATTER, 480)

    @pl.when(jnp.logical_and(first_block, c == 1))
    def _():
        wait_sent(S_SCATTER, 512)

    @pl.when(j < 3)
    def _():
        wait_sent(S_UP, 512)

    @pl.when(j == 0)
    def _():
        wait_sent(S_SKIP, 512)

    for base, near, far in ((0, ROUND_LOW, ROUND_HIGH), (4, ROUND_HIGH, ROUND_LOW)):
        for at, index, count in (
            (0, S_ROUND, len(near)),
            (1, S_RELAY, len(far)),
            (2, S_RELAY, 2 * HEADS - len(near)),
        ):
            if count:
                @pl.when(z == base + at)
                def _():
                    wait_sent(index, 128 * count)


def place(src, dst, buf, sems):
    reads = [pltpu.make_async_copy(src.at[pl.ds(16 * i, 16)], buf.at[pl.ds(16 * i, 16)], sems.at[i]) for i in range(8)]
    writes = [pltpu.make_async_copy(buf.at[pl.ds(16 * i, 16)], dst.at[pl.ds(16 * i, 16)], sems.at[8 + i]) for i in range(8)]
    for copy in reads:
        copy.start()
    for read, write in zip(reads, writes):
        read.wait()
        write.start()
    for copy in writes:
        copy.wait()


def attend(queries, keys, values):
    dma = pltpu.SemaphoreType.DMA
    wide = HEADS * GROUP * HEAD
    result = pl.pallas_call(
        kernel,
        out_shape=jax.ShapeDtypeStruct(queries.shape, BF),
        in_specs=[pl.BlockSpec(memory_space=pl.ANY)] * 3,
        out_specs=pl.BlockSpec(memory_space=pl.ANY),
        scratch_shapes=[
            pltpu.VMEM((CHIP, wide), BF),
            pltpu.VMEM((CHIP, wide), BF),
            pltpu.VMEM((1024, WIDE), BF),
            pltpu.VMEM((1024, WIDE), BF),
            pltpu.VMEM((4, 4, 64, WIDE), BF),
            pltpu.VMEM((4, 4, 64, WIDE), BF),
            pltpu.VMEM((CHIP, WIDE), BF),
            pltpu.VMEM((CHIP, WIDE), BF),
            pltpu.VMEM((CHIP, 1024), F32),
            pltpu.VMEM((CHIP, 1024), F32),
            pltpu.VMEM((CHIP, wide), F32),
            pltpu.VMEM((CHIP, wide), F32),
            pltpu.VMEM((CHIP, wide), F32),
            dma((S_COUNT,)),
            dma((2,)),
            dma((2,)),
            dma((4,)),
            dma((4,)),
            dma((12,)),
            dma((4,)),
            dma((4,)),
            dma(()),
            dma(()),
            pltpu.SemaphoreType.REGULAR,
        ],
        compiler_params=pltpu.CompilerParams(collective_id=0, has_side_effects=True, vmem_limit_bytes=56 << 20),
    )(queries, keys, values)
    return pl.pallas_call(
        place,
        out_shape=jax.ShapeDtypeStruct(queries.shape, BF),
        in_specs=[pl.BlockSpec(memory_space=pl.ANY)],
        out_specs=pl.BlockSpec(memory_space=pl.ANY),
        scratch_shapes=[pltpu.VMEM((128, 8192), BF), pltpu.SemaphoreType.DMA((16,))],
    )(result)


def solution(mesh):
    return jax.shard_map(
        attend,
        mesh=mesh,
        in_specs=(P(("grp", "sp"), None),) * 3,
        out_specs=P(("grp", "sp"), None),
        check_vma=False,
    )
```
